32 devices in a mesh: segment: 2 (over core), seq: 8 (over z, x), mp: 2 (over y).
Axes of the slice: x: 2, y: 2, z: 4, core: 2. Of those that a mesh axis runs over, the one named last changes fastest.
Arguments:
- inputs: bfloat16 [65536, 512], P('seq', 'mp'), may hold values from -6 to 6
- cotangent: bfloat16 [65536, 512], P('seq', 'mp'), may hold values from -0.375 to 0.375
- gate_gain: float32 [2, 512], P('segment', 'mp'), may hold values from 0.3 to 3
- key_gain: float32 [2, 512], P('segment', 'mp'), may hold values from 0.3 to 3
- first_factor: bfloat16 [2, 256, 256, 256], P('segment', 'seq'), may hold values from -0.375 to 0.375
- second_factor: bfloat16 [2, 256, 256, 256], P('segment', 'seq'), may hold values from -0.375 to 0.375
- up_first: bfloat16 [2, 4, 128, 128], P('segment', 'mp'), may hold values from -0.5 to 0.5
- up_second: bfloat16 [2, 4, 128, 512], P('segment', 'mp'), may hold values from -0.5 to 0.5
- down_first: bfloat16 [2, 4, 512, 128], P('segment', 'mp'), may hold values from -0.25 to 0.25
- down_second_weight: bfloat16 [2, 4, 128, 128], P('segment', 'mp'), may hold values from -0.5 to 0.5
Outputs:
- grad_first: float32 [2, 256, 256, 256], P('segment', 'seq', 'mp')
- grad_second: float32 [2, 256, 256, 256], P('segment', 'seq', 'mp')
The draws below stay inside these ranges and needn't reach their ends.
All inputs are finite; a program needn't handle non-finite values.
Results may differ from the reference program's by a relative error of at most 0.024.
Values may be sent and summed in bfloat16 or wider, within the bound.
A program may use at most 192 MiB of HBM per device.

```python
import math
import jax
import jax.numpy as jnp

D = 512
BLOCK = 256
NBLK = 4
LENGTH = 65536
BW = 128
HB = 512
SEGMENTS = 2


def block_levels(key, shape, shards, smallest, high):
    gain = 1.0
    for dim, parts in shards:
        steps = jax.random.uniform(jax.random.fold_in(jax.random.fold_in(key, 6), dim), (parts,), jnp.float32, smallest / len(shards), high / len(shards))
        gain = gain * jnp.repeat(jnp.exp(steps), shape[dim] // parts).reshape((-1,) + (1,) * (len(shape) - 1 - dim))
    return gain


def noise(rng, shape, width, bound, pieces=(), dtype=jnp.bfloat16):
    level = block_levels(rng, shape, pieces, -0.22, 0.18) if pieces else 1.0
    array = jax.random.normal(rng, shape, jnp.float32) * width * level
    return jnp.minimum(jnp.maximum(array, -bound), bound).astype(dtype)


def setup_inputs(seed: int = 0) -> dict:
    key_of = jax.random.split(jax.random.key(seed), 11)
    return {
        "inputs": noise(key_of[0], (LENGTH, D), 1.0, 6.0, ((0, 8), (1, 2))),
        "cotangent": noise(key_of[1], (LENGTH, D), 0.0625, 0.375, ((0, 8), (1, 2))),
        "gate_gain": jnp.clip(jnp.exp(math.log(3.0) - 2.3025851 * jax.random.uniform(key_of[2], (SEGMENTS, D), jnp.float32) ** block_levels(key_of[2], (SEGMENTS, D), ((0, 2), (1, 2)), -0.2, 0.2)), 0.3, 3.0),
        "key_gain": jnp.clip(jnp.exp(math.log(3.0) - 2.3025851 * jax.random.uniform(key_of[3], (SEGMENTS, D), jnp.float32) ** block_levels(key_of[3], (SEGMENTS, D), ((0, 2), (1, 2)), -0.2, 0.2)), 0.3, 3.0),
        "first_factor": noise(key_of[4], (SEGMENTS, BLOCK, BLOCK, BLOCK), BLOCK ** -0.5, 0.375, ((0, 2), (1, 8))),
        "second_factor": noise(key_of[5], (SEGMENTS, BLOCK, BLOCK, BLOCK), BLOCK ** -0.5, 0.375, ((0, 2), (1, 8))),
        "up_first": noise(key_of[6], (SEGMENTS, NBLK, BW, BW), BW ** -0.5, 0.5, ((0, 2), (1, 2))),
        "up_second": noise(key_of[7], (SEGMENTS, NBLK, BW, HB), BW ** -0.5, 0.5, ((0, 2), (1, 2))),
        "down_first": noise(key_of[8], (SEGMENTS, NBLK, HB, BW), HB ** -0.5, 0.25, ((0, 2), (1, 2))),
        "down_second_weight": noise(key_of[9], (SEGMENTS, NBLK, BW, BW), BW ** -0.5, 0.5, ((0, 2), (1, 2))),
    }


def sigmoid_slope(values):
    logistic = jax.nn.sigmoid(values)
    return logistic * (1.0 + values * (1.0 - logistic))


def layer_forward(rows_in, gate_gain, key_gain, first_block, second_block, up_first, up_second, down_first, down_second_weight):
    sequence_length = rows_in.shape[0]
    model_width = rows_in.shape[1]
    block_count = up_first.shape[0]
    block_column_width = up_first.shape[1]
    sub_width = block_column_width // block_count
    rows_grid = rows_in.reshape(BLOCK, BLOCK, model_width).astype(jnp.float32)
    scaled = (rows_grid * key_gain).astype(jnp.bfloat16)
    mixed_rows = jnp.einsum('aoi,aic->aoc', first_block.astype(jnp.float32), scaled.astype(jnp.float32)).astype(jnp.bfloat16)
    turned = jnp.einsum('boi,ibc->obc', second_block.astype(jnp.float32), mixed_rows.astype(jnp.float32)).astype(jnp.bfloat16)
    gate_pre = rows_grid * gate_gain
    hidden_rows = (rows_grid + jax.nn.silu(gate_pre) * turned.astype(jnp.float32)).astype(jnp.bfloat16)
    hidden_rows = hidden_rows.reshape(sequence_length, block_count, block_column_width)
    up_grid = up_first.reshape(block_count, block_column_width, block_count, sub_width).astype(jnp.float32)
    permuted = jnp.einsum('tki,kijc->tjkc', hidden_rows.astype(jnp.float32), up_grid).astype(jnp.bfloat16)
    permuted = permuted.reshape(sequence_length, block_count, block_column_width)
    preact = jnp.einsum('tjq,jqe->tje', permuted.astype(jnp.float32), up_second.astype(jnp.float32))
    active = jax.nn.silu(preact).astype(jnp.bfloat16)
    down_grid = down_first.reshape(block_count, down_first.shape[1], block_count, sub_width).astype(jnp.float32)
    folded_rows = jnp.einsum('tje,jemc->tmjc', active.astype(jnp.float32), down_grid).astype(jnp.bfloat16)
    folded_rows = folded_rows.reshape(sequence_length, block_count, block_column_width)
    output_portion = jnp.einsum('xds,dsl->xdl', folded_rows.astype(jnp.float32), down_second_weight.astype(jnp.float32))
    result = (hidden_rows.astype(jnp.float32) + output_portion).reshape(sequence_length, model_width).astype(jnp.bfloat16)
    return result, (rows_grid, scaled, mixed_rows, turned, preact)


def layer_backward(cot_rows, kept_state, gate_gain, key_gain, first_block, second_block, up_first, up_second, down_first, down_second_weight):
    rows_grid, scaled, mixed_rows, turned, preact = kept_state
    sequence_length = cot_rows.shape[0]
    model_width = cot_rows.shape[1]
    block_count = up_first.shape[0]
    block_column_width = up_first.shape[1]
    sub_width = block_column_width // block_count
    up_grid = up_first.reshape(block_count, block_column_width, block_count, sub_width).astype(jnp.float32)
    down_grid = down_first.reshape(block_count, down_first.shape[1], block_count, sub_width).astype(jnp.float32)
    cotangent_float = cot_rows.astype(jnp.float32)
    backward_folded_rows = jnp.einsum('hsd,sad->hsa', cotangent_float.reshape(sequence_length, block_count, block_column_width), down_second_weight.astype(jnp.float32)).astype(jnp.bfloat16)
    back_grid = backward_folded_rows.reshape(sequence_length, block_count, block_count, sub_width).astype(jnp.float32)
    back_active = jnp.einsum('tmjc,jemc->tje', back_grid, down_grid)
    back_preact = (back_active * sigmoid_slope(preact)).astype(jnp.bfloat16)
    back_perm = jnp.einsum('tje,jqe->tjq', back_preact.astype(jnp.float32), up_second.astype(jnp.float32)).astype(jnp.bfloat16)
    back_perm_grid = back_perm.reshape(sequence_length, block_count, block_count, sub_width).astype(jnp.float32)
    back_ffn = jnp.einsum('tjkc,kijc->tki', back_perm_grid, up_grid).reshape(BLOCK, BLOCK, model_width)
    back_hidden = cotangent_float.reshape(BLOCK, BLOCK, model_width) + back_ffn
    gate_pre = rows_grid * gate_gain
    back_turned = (back_hidden * jax.nn.silu(gate_pre)).astype(jnp.bfloat16)
    second_grad = jnp.einsum('obc,ibc->boi', back_turned.astype(jnp.float32), mixed_rows.astype(jnp.float32))
    back_mixed = jnp.einsum('boi,obc->ibc', second_block.astype(jnp.float32), back_turned.astype(jnp.float32)).astype(jnp.bfloat16)
    first_grad = jnp.einsum('aoc,aic->aoi', back_mixed.astype(jnp.float32), scaled.astype(jnp.float32))
    back_scaled = jnp.einsum('aoi,aoc->aic', first_block.astype(jnp.float32), back_mixed.astype(jnp.float32))
    back_inputs = back_hidden + back_hidden * turned.astype(jnp.float32) * sigmoid_slope(gate_pre) * gate_gain + back_scaled * key_gain
    back_inputs = back_inputs.reshape(sequence_length, model_width).astype(jnp.bfloat16)
    return back_inputs, first_grad, second_grad


def segment_weights(segment_index, gate_gain, key_gain, first_factor, second_factor, up_first, up_second, down_first, down_second_weight):
    return (gate_gain[segment_index], key_gain[segment_index], first_factor[segment_index], second_factor[segment_index],
            up_first[segment_index], up_second[segment_index], down_first[segment_index], down_second_weight[segment_index])


def reference(inputs, cotangent, gate_gain, key_gain, first_factor, second_factor, up_first, up_second, down_first, down_second_weight):
    lower = segment_weights(0, gate_gain, key_gain, first_factor, second_factor, up_first, up_second, down_first, down_second_weight)
    upper = segment_weights(1, gate_gain, key_gain, first_factor, second_factor, up_first, up_second, down_first, down_second_weight)
    middle, kept_lower = layer_forward(inputs, *lower)
    unused_out, kept_upper = layer_forward(middle, *upper)
    passed, first_upper, second_upper = layer_backward(cotangent, kept_upper, *upper)
    ignored, first_lower, second_lower = layer_backward(passed, kept_lower, *lower)
    return jnp.stack([first_lower, first_upper]), jnp.stack([second_lower, second_upper])
```

```python
import functools

import jax
import jax.numpy as jnp
from jax import lax
from jax.experimental import pallas as pl
from jax.experimental.pallas import tpu as pltpu
from jax.sharding import PartitionSpec as P

ALL = ("seq", "segment", "mp")
VMEM_LIMIT = 48 * 1024 * 1024
BF = jnp.bfloat16
F32 = jnp.float32


def logistic(values):
    return 0.5 + 0.5 * jnp.tanh(0.5 * values)


def dot(left, right):
    return lax.dot_general(left, right, (((1,), (0,)), ((), ())), preferred_element_type=F32)


def dot_nt(left, right):
    return lax.dot_general(left, right, (((1,), (1,)), ((), ())), preferred_element_type=F32)


def dot_tn(left, right):
    return lax.dot_general(left, right, (((0,), (0,)), ((), ())), preferred_element_type=F32)


def rows_kernel(x_ref, key_ref, first_ref, mixed_ref):
    scaled = (x_ref[0].astype(F32) * key_ref[...]).astype(BF)
    mixed_ref[0] = dot(first_ref[0], scaled).astype(BF)


def rows_back_kernel(bm_ref, x_ref, key_ref, first_ref, grad_ref, scaled_ref):
    back = bm_ref[0]
    scaled = (x_ref[0].astype(F32) * key_ref[...]).astype(BF)
    grad_ref[0] = dot_nt(back, scaled).astype(BF)
    scaled_ref[0] = dot_tn(first_ref[0], back).astype(BF)


def rows_grad_kernel(bm_ref, x_ref, key_ref, grad_ref):
    scaled = (x_ref[0].astype(F32) * key_ref[...]).astype(BF)
    grad_ref[0] = dot_nt(bm_ref[0], scaled).astype(BF)


def gate_part(mixed, second, x, gate):
    turned = dot(second, mixed).astype(BF).astype(F32)
    gate_pre = x * gate
    sig = logistic(gate_pre)
    hidden = (x + gate_pre * sig * turned).astype(BF)
    return turned, gate_pre, sig, hidden


def forward_kernel(mixed_ref, second_ref, x_ref, gate_ref, up1, up2, down1, down2, out_ref):
    width = up2.shape[1]
    x = x_ref[0].astype(F32)
    _, _, _, hidden = gate_part(mixed_ref[0], second_ref[0], x, gate_ref[...])
    permuted = dot(hidden, up1[...]).astype(BF)
    folded = []
    for j in range(up2.shape[0]):
        pre = dot(permuted[:, j * width : (j + 1) * width], up2[j])
        active = (pre * logistic(pre)).astype(BF)
        folded.append(dot(active, down1[j]).astype(BF))
    folded = jnp.concatenate(folded, axis=1)
    out_ref[0] = (hidden.astype(F32) + dot(folded, down2[...])).astype(BF)


def backward_body(cot, mixed, second, x, gate, up1, up2, down1, down2):
    width = up2.shape[1]
    turned, gate_pre, sig, hidden = gate_part(mixed, second, x, gate)
    permuted = dot(hidden, up1[...]).astype(BF)
    back_fold = dot_nt(cot, down2[...]).astype(BF)
    back_perm = []
    for j in range(up2.shape[0]):
        cols = slice(j * width, (j + 1) * width)
        pre = dot(permuted[:, cols], up2[j])
        back_active = dot_nt(back_fold[:, cols], down1[j])
        act_sig = logistic(pre)
        back_pre = (back_active * (act_sig * (1.0 + pre * (1.0 - act_sig)))).astype(BF)
        back_perm.append(dot_nt(back_pre, up2[j]).astype(BF))
    back_perm = jnp.concatenate(back_perm, axis=1)
    back_hidden = cot.astype(F32) + dot_nt(back_perm, up1[...])
    back_turned = (back_hidden * (gate_pre * sig)).astype(BF)
    second_grad = dot_nt(back_turned, mixed).astype(BF)
    back_mixed = dot_tn(second, back_turned).astype(BF)
    direct = back_hidden + back_hidden * turned * (sig * (1.0 + gate_pre * (1.0 - sig))) * gate
    return second_grad, back_mixed, direct


def upper_kernel(
    cot_ref, mixed_ref, second_ref, x_ref, gate_ref, up1, up2, down1, down2,
    grad_ref, back_ref, direct_ref,
):
    x = x_ref[0].astype(F32)
    grad_ref[0], back_ref[0], direct_ref[0] = backward_body(
        cot_ref[0], mixed_ref[0], second_ref[0], x, gate_ref[...], up1, up2, down1, down2
    )


def lower_kernel(
    direct_ref, scaled_ref, key_ref, mixed_ref, second_ref, x_ref, gate_ref,
    up1, up2, down1, down2, grad_ref, back_ref,
):
    x = x_ref[0].astype(F32)
    cot = (direct_ref[0] + scaled_ref[0].astype(F32) * key_ref[...]).astype(BF)
    grad_ref[0], back_ref[0], _ = backward_body(
        cot, mixed_ref[0], second_ref[0], x, gate_ref[...], up1, up2, down1, down2
    )


def blocked(shape):
    return pl.BlockSpec((1,) + tuple(shape[1:]), lambda n: (n,) + (0,) * (len(shape) - 1))


def whole(shape):
    return pl.BlockSpec(tuple(shape), lambda n: (0,) * len(shape))


def run(kernel, steps, operands, outs, flops):
    moved = sum(a.size * a.dtype.itemsize for a, _ in operands)
    moved += sum(int(jnp.dtype(d).itemsize) * functools.reduce(lambda p, q: p * q, s) for s, d in outs)
    result = pl.pallas_call(
        kernel,
        grid=(steps,),
        in_specs=[(blocked if cut else whole)(a.shape) for a, cut in operands],
        out_specs=[blocked(s) for s, _ in outs],
        out_shape=[jax.ShapeDtypeStruct(s, d) for s, d in outs],
        cost_estimate=pl.CostEstimate(flops=flops, bytes_accessed=moved, transcendentals=0),
        compiler_params=pltpu.CompilerParams(
            vmem_limit_bytes=VMEM_LIMIT, dimension_semantics=("arbitrary",)
        ),
    )(*[a for a, _ in operands])
    return result


def turn(rows):
    own, full, channels = rows.shape
    count = lax.axis_size(ALL)
    sent = jnp.swapaxes(rows, 0, 1)
    got = lax.all_to_all(sent, ALL, split_axis=0, concat_axis=0, tiled=True)
    got = got.reshape(count, full // count, own, channels)
    return jnp.swapaxes(got, 0, 1).reshape(full // count, count * own, channels)


def turn_split(rows):
    own, full, channels = rows.shape
    count = lax.axis_size(ALL)
    parts = lax.axis_size("mp")
    sent = jnp.swapaxes(rows, 0, 1)
    got = lax.all_to_all(sent, ALL, split_axis=0, concat_axis=0, tiled=True)
    got = got.reshape(count // parts, parts, full // count, own, channels)
    return jnp.transpose(got, (2, 0, 3, 1, 4)).reshape(
        full // count, count // parts * own, parts * channels
    )


def spread_pair(first, last):
    layers, blocks, width, _ = first.shape
    sub = width // blocks
    row = lax.broadcasted_iota(jnp.int32, (blocks, width, blocks * width), 1)
    col = lax.broadcasted_iota(jnp.int32, (blocks, width, blocks * width), 2)
    block = lax.broadcasted_iota(jnp.int32, (blocks, width, blocks * width), 0)
    place = (row // sub) * width + block * sub + row % sub
    spread = (col == place).astype(BF)
    up = jnp.einsum("lkir,krn->lkin", first, spread, preferred_element_type=F32)
    down = jnp.einsum("krn,lkrf->lnkf", spread, last, preferred_element_type=F32)
    full = blocks * width
    return up.astype(BF).reshape(layers, full, full), down.astype(BF).reshape(layers, full, full)


def on_device(
    inputs, cotangent, gate_gain, key_gain, first_factor, second_factor,
    up_first, up_second, down_first, down_second_weight,
):
    segments = lax.axis_size("segment")
    parts = lax.axis_size("mp")
    segment = lax.axis_index("segment")
    part = lax.axis_index("mp")
    size = first_factor.shape[2]
    held = first_factor.shape[1]
    channels = inputs.shape[1]
    model = channels * parts
    core_rows = held // segments
    own = core_rows // parts

    gains = jnp.concatenate([key_gain, gate_gain], axis=0)
    gains = lax.all_gather(gains, ("segment", "mp"), axis=0, tiled=False)
    gains = jnp.transpose(gains.reshape(segments, parts, 2, channels), (2, 0, 1, 3))
    gains = gains.reshape(2, segments, 1, model)
    keys, gates = gains[0], gains[1]

    first_all = lax.all_to_all(
        first_factor.reshape(segments, core_rows, size, size), "segment",
        split_axis=0, concat_axis=0, tiled=True,
    )
    first_low = first_all[0]
    first_high = lax.dynamic_slice_in_dim(first_all[1], part * own, own, 0)
    second_mine = lax.dynamic_index_in_dim(
        second_factor.reshape(segments, parts, own, size, size), part, 1, keepdims=False
    )
    second_all = lax.all_to_all(second_mine, "segment", split_axis=0, concat_axis=0, tiled=True)

    core_in = lax.dynamic_slice_in_dim(
        inputs.reshape(held, size, channels), segment * core_rows, core_rows, 0
    )
    core_cot = lax.dynamic_slice_in_dim(
        cotangent.reshape(held, size, channels), segment * core_rows, core_rows, 0
    )

    blocks = up_first.shape[1]
    width = up_first.shape[2]
    packed = jnp.concatenate(
        [
            a.reshape(blocks, -1, width)
            for a in (up_first[0], up_second[0], down_first[0], down_second_weight[0])
        ],
        axis=1,
    )
    packed = lax.all_gather(packed, ("segment", "mp"), axis=0, tiled=False)
    packed = packed.reshape(segments, parts * blocks, -1, width)
    hidden = up_second.shape[3]
    cuts = (0, width, width + hidden, width + 2 * hidden, 2 * width + 2 * hidden)
    piece = [packed[:, :, cuts[n] : cuts[n + 1]] for n in range(4)]
    ups = piece[1].reshape(segments, parts * blocks, width, hidden)
    downs = piece[2]
    wide_up, wide_down = spread_pair(piece[0], piece[3])

    def ffn(layer):
        return [
            (wide_up[layer], False), (ups[layer], False),
            (downs[layer], False), (wide_down[layer], False),
        ]

    grid_rows = (own, size, model)
    grad_shape = (own, size, size)
    cube = 2 * own * size * size * model
    feed = 2 * own * size * model * (2 * model + 2 * hidden)

    key_low = lax.dynamic_slice_in_dim(keys[0], part * channels, channels, 1)
    (mixed_low,) = run(
        rows_kernel, core_rows,
        [(core_in, True), (key_low, False), (first_low, True)],
        [((core_rows, size, channels), BF)], cube,
    )
    mixed_low = turn_split(mixed_low)
    in_cols = turn_split(core_in)
    (middle,) = run(
        forward_kernel, own,
        [(mixed_low, True), (second_all[0], True), (in_cols, True), (gates[0], False)] + ffn(0),
        [(grid_rows, BF)], cube + feed,
    )
    middle_rows = turn(middle)
    (mixed_high,) = run(
        rows_kernel, own,
        [(middle_rows, True), (keys[1], False), (first_high, True)],
        [(grid_rows, BF)], cube,
    )
    mixed_high = turn(mixed_high)
    cot_cols = turn_split(core_cot)
    second_high, back_high, direct = run(
        upper_kernel, own,
        [
            (cot_cols, True), (mixed_high, True), (second_all[1], True),
            (middle, True), (gates[1], False),
        ] + ffn(1),
        [(grad_shape, BF), (grid_rows, BF), (grid_rows, F32)], 3 * cube + 2 * feed,
    )
    back_rows = turn(back_high)
    grad_high, back_scaled = run(
        rows_back_kernel, own,
        [(back_rows, True), (middle_rows, True), (keys[1], False), (first_high, True)],
        [(grad_shape, BF), (grid_rows, BF)], 2 * cube,
    )
    scaled_cols = turn(back_scaled)
    second_low, back_low = run(
        lower_kernel, own,
        [
            (direct, True), (scaled_cols, True), (keys[1], False), (mixed_low, True),
            (second_all[0], True), (in_cols, True), (gates[0], False),
        ] + ffn(0),
        [(grad_shape, BF), (grid_rows, BF)], 3 * cube + 2 * feed,
    )
    in_rows = lax.all_to_all(core_in, "mp", split_axis=0, concat_axis=2, tiled=True)
    low_rows = turn(back_low)
    (grad_low,) = run(
        rows_grad_kernel, own,
        [(low_rows, True), (in_rows, True), (keys[0], False)],
        [(grad_shape, BF)], cube,
    )

    def hand_out(low, high):
        both = jnp.stack([low, high]).reshape(segments, own, parts, size // parts, size)
        both = jnp.swapaxes(both, 1, 2).reshape(segments * parts, own, size // parts, size)
        got = lax.all_to_all(both, ("segment", "mp"), split_axis=0, concat_axis=0, tiled=True)
        return got.reshape(1, held, size // parts, size).astype(F32)

    return hand_out(grad_low, grad_high), hand_out(second_low, second_high)


def solution(mesh):
    placed = (
        P("seq", "mp"),
        P("seq", "mp"),
        P("segment", "mp"),
        P("segment", "mp"),
        P("segment", "seq", None, None),
        P("segment", "seq", None, None),
        P("segment", "mp", None, None),
        P("segment", "mp", None, None),
        P("segment", "mp", None, None),
        P("segment", "mp", None, None),
    )
    return jax.shard_map(
        on_device,
        mesh=mesh,
        in_specs=placed,
        out_specs=(P("segment", "seq", "mp", None), P("segment", "seq", "mp", None)),
        check_vma=False,
    )
```

```python
import functools

import jax
import jax.numpy as jnp
from jax import lax
from jax.experimental import pallas as pl
from jax.experimental.pallas import tpu as pltpu
from jax.sharding import PartitionSpec as P

ALL = ("seq", "segment", "mp")
VMEM_LIMIT = 48 * 1024 * 1024
BF = jnp.bfloat16
F32 = jnp.float32


def logistic(values):
    return 0.5 + 0.5 * jnp.tanh(0.5 * values)


def dot(left, right):
    return lax.dot_general(left, right, (((1,), (0,)), ((), ())), preferred_element_type=F32)


def dot_nt(left, right):
    return lax.dot_general(left, right, (((1,), (1,)), ((), ())), preferred_element_type=F32)


def dot_tn(left, right):
    return lax.dot_general(left, right, (((0,), (0,)), ((), ())), preferred_element_type=F32)


def column(ref):
    if len(ref.shape) == 3:
        return ref[0]
    senders, parts, _, own, channels = ref.shape
    return jnp.concatenate(
        [ref[:, n, 0].reshape(senders * own, channels) for n in range(parts)], axis=1
    )


def rows_kernel(x_ref, key_ref, first_ref, mixed_ref):
    scaled = (x_ref[0].astype(F32) * key_ref[...]).astype(BF)
    mixed_ref[0] = dot(first_ref[0], scaled).astype(BF)


def rows_back_kernel(bm_ref, x_ref, key_ref, first_ref, grad_ref, scaled_ref):
    back = bm_ref[0]
    scaled = (x_ref[0].astype(F32) * key_ref[...]).astype(BF)
    grad_ref[0] = dot_nt(back, scaled).astype(BF)
    scaled_ref[0] = dot_tn(first_ref[0], back).astype(BF)


def rows_grad_kernel(bm_ref, x_ref, key_ref, grad_ref):
    scaled = (x_ref[0].astype(F32) * key_ref[...]).astype(BF)
    grad_ref[0] = dot_nt(bm_ref[0], scaled).astype(BF)


def gate_part(mixed, second, x, gate):
    turned = dot(second, mixed).astype(BF).astype(F32)
    gate_pre = x * gate
    sig = logistic(gate_pre)
    hidden = (x + gate_pre * sig * turned).astype(BF)
    return turned, gate_pre, sig, hidden


def forward_kernel(mixed_ref, second_ref, x_ref, gate_ref, up1, up2, down1, down2, out_ref):
    width = up2.shape[1]
    x = column(x_ref).astype(F32)
    _, _, _, hidden = gate_part(column(mixed_ref), second_ref[0], x, gate_ref[...])
    permuted = dot(hidden, up1[...]).astype(BF)
    folded = []
    for j in range(up2.shape[0]):
        pre = dot(permuted[:, j * width : (j + 1) * width], up2[j])
        active = (pre * logistic(pre)).astype(BF)
        folded.append(dot(active, down1[j]).astype(BF))
    folded = jnp.concatenate(folded, axis=1)
    out_ref[0] = (hidden.astype(F32) + dot(folded, down2[...])).astype(BF)


def backward_body(cot, mixed, second, x, gate, up1, up2, down1, down2):
    width = up2.shape[1]
    turned, gate_pre, sig, hidden = gate_part(mixed, second, x, gate)
    permuted = dot(hidden, up1[...]).astype(BF)
    back_fold = dot_nt(cot, down2[...]).astype(BF)
    back_perm = []
    for j in range(up2.shape[0]):
        cols = slice(j * width, (j + 1) * width)
        pre = dot(permuted[:, cols], up2[j])
        back_active = dot_nt(back_fold[:, cols], down1[j])
        act_sig = logistic(pre)
        back_pre = (back_active * (act_sig * (1.0 + pre * (1.0 - act_sig)))).astype(BF)
        back_perm.append(dot_nt(back_pre, up2[j]).astype(BF))
    back_perm = jnp.concatenate(back_perm, axis=1)
    back_hidden = cot.astype(F32) + dot_nt(back_perm, up1[...])
    back_turned = (back_hidden * (gate_pre * sig)).astype(BF)
    second_grad = dot_nt(back_turned, mixed).astype(BF)
    back_mixed = dot_tn(second, back_turned).astype(BF)
    direct = back_hidden + back_hidden * turned * (sig * (1.0 + gate_pre * (1.0 - sig))) * gate
    return second_grad, back_mixed, direct


def upper_kernel(
    cot_ref, mixed_ref, second_ref, x_ref, gate_ref, up1, up2, down1, down2,
    grad_ref, back_ref, direct_ref,
):
    x = x_ref[0].astype(F32)
    grad_ref[0], back_ref[0], direct_ref[0] = backward_body(
        column(cot_ref), mixed_ref[0], second_ref[0], x, gate_ref[...], up1, up2, down1, down2
    )


def lower_kernel(
    direct_ref, scaled_ref, key_ref, mixed_ref, second_ref, x_ref, gate_ref,
    up1, up2, down1, down2, grad_ref, back_ref,
):
    x = column(x_ref).astype(F32)
    cot = (direct_ref[0] + scaled_ref[0].astype(F32) * key_ref[...]).astype(BF)
    grad_ref[0], back_ref[0], _ = backward_body(
        cot, column(mixed_ref), second_ref[0], x, gate_ref[...], up1, up2, down1, down2
    )


def blocked(shape):
    return pl.BlockSpec((1,) + tuple(shape[1:]), lambda n: (n,) + (0,) * (len(shape) - 1))


def whole(shape):
    return pl.BlockSpec(tuple(shape), lambda n: (0,) * len(shape))


def spec(shape, how):
    if how is True and len(shape) == 5:
        return pl.BlockSpec((shape[0], shape[1], 1) + tuple(shape[3:]), lambda n: (0, 0, n, 0, 0))
    if how is True:
        return blocked(shape)
    if how is False:
        return whole(shape)
    layer = how[0]
    return pl.BlockSpec((None,) + tuple(shape[1:]), lambda n: (layer,) + (0,) * (len(shape) - 1))


def run(kernel, steps, operands, outs, flops):
    moved = sum(a.size * a.dtype.itemsize for a, _ in operands)
    moved += sum(int(jnp.dtype(d).itemsize) * functools.reduce(lambda p, q: p * q, s) for s, d in outs)
    result = pl.pallas_call(
        kernel,
        grid=(steps,),
        in_specs=[spec(a.shape, how) for a, how in operands],
        out_specs=[blocked(s) for s, _ in outs],
        out_shape=[jax.ShapeDtypeStruct(s, d) for s, d in outs],
        cost_estimate=pl.CostEstimate(flops=flops, bytes_accessed=moved, transcendentals=0),
        compiler_params=pltpu.CompilerParams(
            vmem_limit_bytes=VMEM_LIMIT, dimension_semantics=("arbitrary",)
        ),
    )(*[a for a, _ in operands])
    return result


def turn(rows):
    own, full, channels = rows.shape
    count = lax.axis_size(ALL)
    sent = jnp.swapaxes(rows, 0, 1)
    got = lax.all_to_all(sent, ALL, split_axis=0, concat_axis=0, tiled=True)
    got = got.reshape(count, full // count, own, channels)
    return jnp.swapaxes(got, 0, 1).reshape(full // count, count * own, channels)


def order_columns(rows):
    return jnp.swapaxes(rows, 0, 1)


def turn_split(sent):
    full, own, channels = sent.shape
    count = lax.axis_size(ALL)
    parts = lax.axis_size("mp")
    got = lax.all_to_all(sent, ALL, split_axis=0, concat_axis=0, tiled=True)
    got = got.reshape(count // parts, parts, full // count, own, channels)
    if own % 16 == 0:
        return got
    return jnp.transpose(got, (2, 0, 3, 1, 4)).reshape(
        full // count, count // parts * own, parts * channels
    )


def swap(pieces, axis):
    count = lax.axis_size(axis)
    me = lax.axis_index(axis)

    def chosen(index):
        piece = pieces[0]
        for n in range(1, count):
            piece = jnp.where(index == n, pieces[n], piece)
        return piece

    held = [chosen(me)]
    for shift in range(1, count):
        route = [(n, (n + shift) % count) for n in range(count)]
        held.append(lax.ppermute(chosen((me + shift) % count), axis, route))
    result = []
    for source in range(count):
        piece = held[0]
        for shift in range(1, count):
            piece = jnp.where((me - source) % count == shift, held[shift], piece)
        result.append(piece)
    return result


def spread_pair(first, last):
    layers, blocks, width, _ = first.shape
    sub = width // blocks
    row = lax.broadcasted_iota(jnp.int32, (blocks, width, blocks * width), 1)
    col = lax.broadcasted_iota(jnp.int32, (blocks, width, blocks * width), 2)
    block = lax.broadcasted_iota(jnp.int32, (blocks, width, blocks * width), 0)
    place = (row // sub) * width + block * sub + row % sub
    spread = (col == place).astype(BF)
    up = jnp.einsum("lkir,krn->lkin", first, spread, preferred_element_type=F32)
    down = jnp.einsum("krn,lkrf->lnkf", spread, last, preferred_element_type=F32)
    full = blocks * width
    return up.astype(BF).reshape(layers, full, full), down.astype(BF).reshape(layers, full, full)


def on_device(
    inputs, cotangent, gate_gain, key_gain, first_factor, second_factor,
    up_first, up_second, down_first, down_second_weight,
):
    segments = lax.axis_size("segment")
    parts = lax.axis_size("mp")
    segment = lax.axis_index("segment")
    part = lax.axis_index("mp")
    size = first_factor.shape[2]
    held = first_factor.shape[1]
    channels = inputs.shape[1]
    model = channels * parts
    core_rows = held // segments
    own = core_rows // parts

    gains = jnp.concatenate([key_gain, gate_gain], axis=0)
    gains = lax.all_gather(gains, ("segment", "mp"), axis=0, tiled=False)
    gains = jnp.transpose(gains.reshape(segments, parts, 2, channels), (2, 0, 1, 3))
    gains = gains.reshape(2, segments, 1, model)
    keys, gates = gains[0], gains[1]

    first_cut = first_factor.reshape(segments, core_rows, size, size)
    first_low, first_high = swap([first_cut[n] for n in range(segments)], "segment")
    first_high = lax.dynamic_slice_in_dim(first_high, part * own, own, 0)
    second_mine = lax.dynamic_index_in_dim(
        second_factor.reshape(segments, parts, own, size, size), part, 1, keepdims=False
    )
    second_low_block, second_high_block = swap(
        [second_mine[n] for n in range(segments)], "segment"
    )

    core_in = lax.dynamic_slice_in_dim(
        inputs.reshape(held, size, channels), segment * core_rows, core_rows, 0
    )
    core_cot = lax.dynamic_slice_in_dim(
        cotangent.reshape(held, size, channels), segment * core_rows, core_rows, 0
    )

    blocks = up_first.shape[1]
    width = up_first.shape[2]
    packed = jnp.concatenate(
        [
            a.reshape(blocks, -1, width)
            for a in (up_first[0], up_second[0], down_first[0], down_second_weight[0])
        ],
        axis=1,
    )
    packed = lax.all_gather(packed, ("segment", "mp"), axis=0, tiled=False)
    packed = packed.reshape(segments, parts * blocks, -1, width)
    hidden = up_second.shape[3]
    cuts = (0, width, width + hidden, width + 2 * hidden, 2 * width + 2 * hidden)
    piece = [packed[:, :, cuts[n] : cuts[n + 1]] for n in range(4)]
    ups = piece[1].reshape(segments, parts * blocks, width, hidden)
    downs = piece[2]
    wide_up, wide_down = spread_pair(piece[0], piece[3])

    def ffn(layer):
        return [
            (wide_up, (layer,)), (ups, (layer,)), (downs, (layer,)), (wide_down, (layer,)),
        ]

    grid_rows = (own, size, model)
    grad_shape = (own, size, size)
    cube = 2 * own * size * size * model
    feed = 2 * own * size * model * (2 * model + 2 * hidden)

    key_low = lax.dynamic_slice_in_dim(keys[0], part * channels, channels, 1)
    (mixed_low,) = run(
        rows_kernel, core_rows,
        [(core_in, True), (key_low, False), (first_low, True)],
        [((core_rows, size, channels), BF)], cube,
    )
    in_cols = turn_split(order_columns(core_in))
    mixed_low, in_cols = lax.optimization_barrier((order_columns(mixed_low), in_cols))
    mixed_low = turn_split(mixed_low)
    cot_cols = turn_split(order_columns(core_cot))
    (middle,) = run(
        forward_kernel, own,
        [(mixed_low, True), (second_low_block, True), (in_cols, True), (gates[0], False)] + ffn(0),
        [(grid_rows, BF)], cube + feed,
    )
    middle, cot_cols = lax.optimization_barrier((middle, cot_cols))
    middle_rows = turn(middle)
    (mixed_high,) = run(
        rows_kernel, own,
        [(middle_rows, True), (keys[1], False), (first_high, True)],
        [(grid_rows, BF)], cube,
    )
    mixed_high = turn(mixed_high)
    second_high, back_high, direct = run(
        upper_kernel, own,
        [
            (cot_cols, True), (mixed_high, True), (second_high_block, True),
            (middle, True), (gates[1], False),
        ] + ffn(1),
        [(grad_shape, BF), (grid_rows, BF), (grid_rows, F32)], 3 * cube + 2 * feed,
    )
    back_rows = turn(back_high)
    grad_high, back_scaled = run(
        rows_back_kernel, own,
        [(back_rows, True), (middle_rows, True), (keys[1], False), (first_high, True)],
        [(grad_shape, BF), (grid_rows, BF)], 2 * cube,
    )
    scaled_cols = turn(back_scaled)
    second_low, back_low = run(
        lower_kernel, own,
        [
            (direct, True), (scaled_cols, True), (keys[1], False), (mixed_low, True),
            (second_low_block, True), (in_cols, True), (gates[0], False),
        ] + ffn(0),
        [(grad_shape, BF), (grid_rows, BF)], 3 * cube + 2 * feed,
    )
    in_cut = core_in.reshape(parts, own, size, channels)
    in_rows = jnp.concatenate(swap([in_cut[n] for n in range(parts)], "mp"), axis=2)
    low_rows = turn(back_low)
    (grad_low,) = run(
        rows_grad_kernel, own,
        [(low_rows, True), (in_rows, True), (keys[0], False)],
        [(grad_shape, BF)], cube,
    )

    def halves(grad):
        cut = grad.reshape(own, parts, size // parts, size)
        return jnp.stack(swap([cut[:, n] for n in range(parts)], "mp"))

    def hand_out(low, high):
        got = jnp.stack(swap([halves(low), halves(high)], "segment"))
        return got.reshape(1, held, size // parts, size).astype(F32)

    return hand_out(grad_low, grad_high), hand_out(second_low, second_high)


def solution(mesh):
    placed = (
        P("seq", "mp"),
        P("seq", "mp"),
        P("segment", "mp"),
        P("segment", "mp"),
        P("segment", "seq", None, None),
        P("segment", "seq", None, None),
        P("segment", "mp", None, None),
        P("segment", "mp", None, None),
        P("segment", "mp", None, None),
        P("segment", "mp", None, None),
    )
    return jax.shard_map(
        on_device,
        mesh=mesh,
        in_specs=placed,
        out_specs=(P("segment", "seq", "mp", None), P("segment", "seq", "mp", None)),
        check_vma=False,
    )
```

```python
import functools

import jax
import jax.numpy as jnp
from jax import lax
from jax.experimental import pallas as pl
from jax.experimental.pallas import tpu as pltpu
from jax.sharding import PartitionSpec as P

ALL = ("seq", "segment", "mp")
VMEM_LIMIT = 48 * 1024 * 1024
BF = jnp.bfloat16
F32 = jnp.float32


def logistic(values):
    return 0.5 + 0.5 * jnp.tanh(0.5 * values)


def dot(left, right):
    return lax.dot_general(left, right, (((1,), (0,)), ((), ())), preferred_element_type=F32)


def dot_nt(left, right):
    return lax.dot_general(left, right, (((1,), (1,)), ((), ())), preferred_element_type=F32)


def dot_tn(left, right):
    return lax.dot_general(left, right, (((0,), (0,)), ((), ())), preferred_element_type=F32)


def column(ref):
    if len(ref.shape) == 3:
        return ref[0]
    senders, parts, _, own, channels = ref.shape
    return jnp.concatenate(
        [ref[:, n, 0].reshape(senders * own, channels) for n in range(parts)], axis=1
    )


def rows_kernel(x_ref, key_ref, first_ref, mixed_ref):
    scaled = (x_ref[0].astype(F32) * key_ref[...]).astype(BF)
    mixed_ref[0] = dot(first_ref[0], scaled).astype(BF)


def rows_back_kernel(bm_ref, x_ref, key_ref, first_ref, grad_ref, scaled_ref):
    back = bm_ref[0]
    scaled = (x_ref[0].astype(F32) * key_ref[...]).astype(BF)
    grad_ref[0] = dot_nt(back, scaled).astype(BF)
    scaled_ref[0] = dot_tn(first_ref[0], back).astype(BF)


def rows_grad_kernel(bm_ref, x_ref, key_ref, grad_ref):
    scaled = (x_ref[0].astype(F32) * key_ref[...]).astype(BF)
    grad_ref[0] = dot_nt(bm_ref[0], scaled).astype(BF)


def gate_part(mixed, second, x, gate):
    turned = dot(second, mixed).astype(BF).astype(F32)
    gate_pre = x * gate
    sig = logistic(gate_pre)
    hidden = (x + gate_pre * sig * turned).astype(BF)
    return turned, gate_pre, sig, hidden


def forward_kernel(mixed_ref, second_ref, x_ref, gate_ref, up1, up2, down1, down2, out_ref, sent):
    width = up2.shape[1]
    x = column(x_ref).astype(F32)
    _, _, _, hidden = gate_part(column(mixed_ref), second_ref[0], x, gate_ref[...])
    permuted = dot(hidden, up1[...]).astype(BF)
    folded = []
    for j in range(up2.shape[0]):
        pre = dot(permuted[:, j * width : (j + 1) * width], up2[j])
        active = (pre * logistic(pre)).astype(BF)
        folded.append(dot(active, down1[j]).astype(BF))
    folded = jnp.concatenate(folded, axis=1)
    result = (hidden.astype(F32) + dot(folded, down2[...])).astype(BF)
    out_ref[0] = result
    sent[0] = result


def backward_body(cot, mixed, second, x, gate, up1, up2, down1, down2):
    width = up2.shape[1]
    turned, gate_pre, sig, hidden = gate_part(mixed, second, x, gate)
    permuted = dot(hidden, up1[...]).astype(BF)
    back_fold = dot_nt(cot, down2[...]).astype(BF)
    back_perm = []
    for j in range(up2.shape[0]):
        cols = slice(j * width, (j + 1) * width)
        pre = dot(permuted[:, cols], up2[j])
        back_active = dot_nt(back_fold[:, cols], down1[j])
        act_sig = logistic(pre)
        back_pre = (back_active * (act_sig * (1.0 + pre * (1.0 - act_sig)))).astype(BF)
        back_perm.append(dot_nt(back_pre, up2[j]).astype(BF))
    back_perm = jnp.concatenate(back_perm, axis=1)
    back_hidden = cot.astype(F32) + dot_nt(back_perm, up1[...])
    back_turned = (back_hidden * (gate_pre * sig)).astype(BF)
    second_grad = dot_nt(back_turned, mixed).astype(BF)
    back_mixed = dot_tn(second, back_turned).astype(BF)
    direct = back_hidden + back_hidden * turned * (sig * (1.0 + gate_pre * (1.0 - sig))) * gate
    return second_grad, back_mixed, direct


def upper_kernel(
    cot_ref, mixed_ref, second_ref, x_ref, gate_ref, up1, up2, down1, down2,
    grad_ref, direct_ref, back_ref,
):
    x = x_ref[0].astype(F32)
    grad_ref[0], back_ref[0], direct_ref[0] = backward_body(
        column(cot_ref), mixed_ref[0], second_ref[0], x, gate_ref[...], up1, up2, down1, down2
    )


def lower_kernel(
    direct_ref, scaled_ref, key_ref, mixed_ref, second_ref, x_ref, gate_ref,
    up1, up2, down1, down2, grad_ref, back_ref,
):
    x = column(x_ref).astype(F32)
    cot = (direct_ref[0] + scaled_ref[0].astype(F32) * key_ref[...]).astype(BF)
    grad_ref[0], back_ref[0], _ = backward_body(
        cot, column(mixed_ref), second_ref[0], x, gate_ref[...], up1, up2, down1, down2
    )


def blocked(shape):
    return pl.BlockSpec((1,) + tuple(shape[1:]), lambda n: (n,) + (0,) * (len(shape) - 1))


def whole(shape):
    return pl.BlockSpec(tuple(shape), lambda n: (0,) * len(shape))


def spec(shape, how):
    if how is True and len(shape) == 5:
        return pl.BlockSpec((shape[0], shape[1], 1) + tuple(shape[3:]), lambda n: (0, 0, n, 0, 0))
    if how is True:
        return blocked(shape)
    if how is False:
        return whole(shape)
    layer = how[0]
    return pl.BlockSpec((None,) + tuple(shape[1:]), lambda n: (layer,) + (0,) * (len(shape) - 1))


def run(kernel, steps, operands, outs, flops):
    moved = sum(a.size * a.dtype.itemsize for a, _ in operands)
    moved += sum(int(jnp.dtype(d).itemsize) * functools.reduce(lambda p, q: p * q, s) for s, d in outs)
    result = pl.pallas_call(
        kernel,
        grid=(steps,),
        in_specs=[spec(a.shape, how) for a, how in operands],
        out_specs=[blocked(s) for s, _ in outs],
        out_shape=[jax.ShapeDtypeStruct(s, d) for s, d in outs],
        cost_estimate=pl.CostEstimate(flops=flops, bytes_accessed=moved, transcendentals=0),
        compiler_params=pltpu.CompilerParams(
            vmem_limit_bytes=VMEM_LIMIT, dimension_semantics=("arbitrary",)
        ),
    )(*[a for a, _ in operands])
    return result


class Outgoing:
    def __init__(self, ref, step):
        self.ref, self.step = ref, step

    def __setitem__(self, _, rows):
        count, _, own, channels = self.ref.shape
        self.ref[:, self.step] = rows.reshape(count, own, channels)


def run_and_turn(kernel, steps, operands, outs, flops, channels, collective_id):
    parts, segments, seqs = lax.axis_size("mp"), lax.axis_size("segment"), lax.axis_size("seq")
    count = parts * segments * seqs
    own = steps
    group = max(1, own // 4)
    n_in, n_out = len(operands), len(outs)

    def body(*refs):
        got = refs[n_in + n_out]
        slots, send_sem, recv_sem, own_sem = refs[n_in + n_out + 1 :]
        step = pl.program_id(0)
        me = (lax.axis_index("seq") * segments + lax.axis_index("segment")) * parts + lax.axis_index("mp")

        def place(k):
            device = lax.rem(me + k, count)
            return device, {
                "segment": lax.rem(device // parts, segments),
                "seq": device // (parts * segments),
                "mp": lax.rem(device, parts),
            }

        barrier = pltpu.get_barrier_semaphore()

        @pl.when(step == 0)
        def _():
            @pl.loop(1, count)
            def _(k):
                pl.semaphore_signal(
                    barrier, inc=1, device_id=place(k)[1], device_id_type=pl.DeviceIdType.MESH
                )

        kernel(*refs[: n_in + n_out], Outgoing(slots, step))

        @pl.when(step == group - 1)
        def _():
            pl.semaphore_wait(barrier, count - 1)

        @pl.when(lax.rem(step, group) == group - 1)
        def _():
            base = step - (group - 1)
            target = got.at[pl.ds(me * own + base, group)]

            @pl.loop(1, count)
            def _(k):
                device, where = place(k)
                pltpu.make_async_remote_copy(
                    src_ref=slots.at[device, pl.ds(base, group)],
                    dst_ref=target,
                    send_sem=send_sem,
                    recv_sem=recv_sem,
                    device_id=where,
                    device_id_type=pl.DeviceIdType.MESH,
                ).start()

        @pl.when(step == own - 1)
        def _():
            mine = pltpu.make_async_copy(slots.at[me], got.at[pl.ds(me * own, own)], own_sem)
            mine.start()
            mine.wait()
            others = slots.at[pl.ds(0, count - 1)]
            pltpu.make_async_copy(others, others, send_sem).wait()
            arrived = got.at[pl.ds(0, (count - 1) * own)]
            pltpu.make_async_copy(arrived, arrived, recv_sem).wait()

    moved = sum(a.size * a.dtype.itemsize for a, _ in operands)
    result = pl.pallas_call(
        body,
        grid=(steps,),
        in_specs=[spec(a.shape, how) for a, how in operands],
        out_specs=[blocked(s) for s, _ in outs] + [pl.BlockSpec(memory_space=pl.ANY)],
        out_shape=[jax.ShapeDtypeStruct(s, d) for s, d in outs]
        + [jax.ShapeDtypeStruct((count * own, own, channels), BF)],
        scratch_shapes=[
            pltpu.VMEM((count, own, own, channels), BF),
            pltpu.SemaphoreType.DMA,
            pltpu.SemaphoreType.DMA,
            pltpu.SemaphoreType.DMA,
        ],
        cost_estimate=pl.CostEstimate(
            flops=flops, bytes_accessed=moved + 150_000_000, transcendentals=0
        ),
        compiler_params=pltpu.CompilerParams(
            vmem_limit_bytes=VMEM_LIMIT, dimension_semantics=("arbitrary",),
            collective_id=collective_id, has_side_effects=True,
        ),
    )(*[a for a, _ in operands])
    return list(result[:-1]) + [jnp.swapaxes(result[-1], 0, 1)]


def order_columns(rows):
    return jnp.swapaxes(rows, 0, 1)


def turn_split(sent):
    full, own, channels = sent.shape
    count = lax.axis_size(ALL)
    parts = lax.axis_size("mp")
    got = lax.all_to_all(sent, ALL, split_axis=0, concat_axis=0, tiled=True)
    got = got.reshape(count // parts, parts, full // count, own, channels)
    if own % 16 == 0:
        return got
    return jnp.transpose(got, (2, 0, 3, 1, 4)).reshape(
        full // count, count // parts * own, parts * channels
    )


def swap(pieces, axis):
    count = lax.axis_size(axis)
    me = lax.axis_index(axis)

    def chosen(index):
        piece = pieces[0]
        for n in range(1, count):
            piece = jnp.where(index == n, pieces[n], piece)
        return piece

    held = [chosen(me)]
    for shift in range(1, count):
        route = [(n, (n + shift) % count) for n in range(count)]
        held.append(lax.ppermute(chosen((me + shift) % count), axis, route))
    result = []
    for source in range(count):
        piece = held[0]
        for shift in range(1, count):
            piece = jnp.where((me - source) % count == shift, held[shift], piece)
        result.append(piece)
    return result


def spread_pair(first, last):
    layers, blocks, width, _ = first.shape
    sub = width // blocks
    row = lax.broadcasted_iota(jnp.int32, (blocks, width, blocks * width), 1)
    col = lax.broadcasted_iota(jnp.int32, (blocks, width, blocks * width), 2)
    block = lax.broadcasted_iota(jnp.int32, (blocks, width, blocks * width), 0)
    place = (row // sub) * width + block * sub + row % sub
    spread = (col == place).astype(BF)
    up = jnp.einsum("lkir,krn->lkin", first, spread, preferred_element_type=F32)
    down = jnp.einsum("krn,lkrf->lnkf", spread, last, preferred_element_type=F32)
    full = blocks * width
    return up.astype(BF).reshape(layers, full, full), down.astype(BF).reshape(layers, full, full)


def on_device(
    inputs, cotangent, gate_gain, key_gain, first_factor, second_factor,
    up_first, up_second, down_first, down_second_weight,
):
    segments = lax.axis_size("segment")
    parts = lax.axis_size("mp")
    segment = lax.axis_index("segment")
    part = lax.axis_index("mp")
    size = first_factor.shape[2]
    held = first_factor.shape[1]
    channels = inputs.shape[1]
    model = channels * parts
    core_rows = held // segments
    own = core_rows // parts

    gains = jnp.concatenate([key_gain, gate_gain], axis=0)
    gains = lax.all_gather(gains, ("segment", "mp"), axis=0, tiled=False)
    gains = jnp.transpose(gains.reshape(segments, parts, 2, channels), (2, 0, 1, 3))
    gains = gains.reshape(2, segments, 1, model)
    keys, gates = gains[0], gains[1]

    first_cut = first_factor.reshape(segments, core_rows, size, size)
    first_low, first_high = swap([first_cut[n] for n in range(segments)], "segment")
    first_high = lax.dynamic_slice_in_dim(first_high, part * own, own, 0)
    second_mine = lax.dynamic_index_in_dim(
        second_factor.reshape(segments, parts, own, size, size), part, 1, keepdims=False
    )
    second_low_block, second_high_block = swap(
        [second_mine[n] for n in range(segments)], "segment"
    )

    core_in = lax.dynamic_slice_in_dim(
        inputs.reshape(held, size, channels), segment * core_rows, core_rows, 0
    )
    core_cot = lax.dynamic_slice_in_dim(
        cotangent.reshape(held, size, channels), segment * core_rows, core_rows, 0
    )

    blocks = up_first.shape[1]
    width = up_first.shape[2]
    packed = jnp.concatenate(
        [
            a.reshape(blocks, -1, width)
            for a in (up_first[0], up_second[0], down_first[0], down_second_weight[0])
        ],
        axis=1,
    )
    packed = lax.all_gather(packed, ("segment", "mp"), axis=0, tiled=False)
    packed = packed.reshape(segments, parts * blocks, -1, width)
    hidden = up_second.shape[3]
    cuts = (0, width, width + hidden, width + 2 * hidden, 2 * width + 2 * hidden)
    piece = [packed[:, :, cuts[n] : cuts[n + 1]] for n in range(4)]
    ups = piece[1].reshape(segments, parts * blocks, width, hidden)
    downs = piece[2]
    wide_up, wide_down = spread_pair(piece[0], piece[3])

    def ffn(layer):
        return [
            (wide_up, (layer,)), (ups, (layer,)), (downs, (layer,)), (wide_down, (layer,)),
        ]

    grid_rows = (own, size, model)
    grad_shape = (own, size, size)
    cube = 2 * own * size * size * model
    feed = 2 * own * size * model * (2 * model + 2 * hidden)

    def halves(grad):
        cut = grad.reshape(own, parts, size // parts, size)
        return jnp.stack(swap([cut[:, n] for n in range(parts)], "mp"))

    key_low = lax.dynamic_slice_in_dim(keys[0], part * channels, channels, 1)
    (mixed_low,) = run(
        rows_kernel, core_rows,
        [(core_in, True), (key_low, False), (first_low, True)],
        [((core_rows, size, channels), BF)], cube,
    )
    in_cols = turn_split(order_columns(core_in))
    mixed_low, in_cols = lax.optimization_barrier((order_columns(mixed_low), in_cols))
    mixed_low = turn_split(mixed_low)
    cot_cols = turn_split(order_columns(core_cot))
    middle, middle_rows = run_and_turn(
        forward_kernel, own,
        [(mixed_low, True), (second_low_block, True), (in_cols, True), (gates[0], False)] + ffn(0),
        [(grid_rows, BF)], cube + feed, model, 0,
    )
    middle_rows, cot_cols = lax.optimization_barrier((middle_rows, cot_cols))
    (mixed_high,) = run_and_turn(
        rows_kernel, own,
        [(middle_rows, True), (keys[1], False), (first_high, True)],
        [], cube, model, 1,
    )
    second_high, direct, back_rows = run_and_turn(
        upper_kernel, own,
        [
            (cot_cols, True), (mixed_high, True), (second_high_block, True),
            (middle, True), (gates[1], False),
        ] + ffn(1),
        [(grad_shape, BF), (grid_rows, F32)], 3 * cube + 2 * feed, model, 2,
    )
    grad_high, scaled_cols = run_and_turn(
        rows_back_kernel, own,
        [(back_rows, True), (middle_rows, True), (keys[1], False), (first_high, True)],
        [(grad_shape, BF)], 2 * cube, model, 3,
    )
    in_cut = core_in.reshape(parts, own, size, channels)
    in_rows = jnp.concatenate(swap([in_cut[n] for n in range(parts)], "mp"), axis=2)
    second_high = halves(second_high)
    scaled_cols, in_rows, second_high = lax.optimization_barrier(
        (scaled_cols, in_rows, second_high)
    )
    grad_high = halves(grad_high)
    second_low, low_rows = run_and_turn(
        lower_kernel, own,
        [
            (direct, True), (scaled_cols, True), (keys[1], False), (mixed_low, True),
            (second_low_block, True), (in_cols, True), (gates[0], False),
        ] + ffn(0),
        [(grad_shape, BF)], 3 * cube + 2 * feed, model, 4,
    )
    low_rows, grad_high = lax.optimization_barrier((low_rows, grad_high))
    (grad_low,) = run(
        rows_grad_kernel, own,
        [(low_rows, True), (in_rows, True), (keys[0], False)],
        [(grad_shape, BF)], cube,
    )

    def hand_out(low, high):
        got = jnp.stack(swap([halves(low), high], "segment"))
        return got.reshape(1, held, size // parts, size).astype(F32)

    return hand_out(grad_low, grad_high), hand_out(second_low, second_high)


def solution(mesh):
    placed = (
        P("seq", "mp"),
        P("seq", "mp"),
        P("segment", "mp"),
        P("segment", "mp"),
        P("segment", "seq", None, None),
        P("segment", "seq", None, None),
        P("segment", "mp", None, None),
        P("segment", "mp", None, None),
        P("segment", "mp", None, None),
        P("segment", "mp", None, None),
    )
    return jax.shard_map(
        on_device,
        mesh=mesh,
        in_specs=placed,
        out_specs=(P("segment", "seq", "mp", None), P("segment", "seq", "mp", None)),
        check_vma=False,
    )
```

```python
import functools

import jax
import jax.numpy as jnp
from jax import lax
from jax.experimental import pallas as pl
from jax.experimental.pallas import tpu as pltpu
from jax.sharding import PartitionSpec as P

ALL = ("seq", "segment", "mp")
VMEM_LIMIT = 48 * 1024 * 1024
BF = jnp.bfloat16
F32 = jnp.float32


def logistic(values):
    return 0.5 + 0.5 * jnp.tanh(0.5 * values)


def dot(left, right):
    return lax.dot_general(left, right, (((1,), (0,)), ((), ())), preferred_element_type=F32)


def dot_nt(left, right):
    return lax.dot_general(left, right, (((1,), (1,)), ((), ())), preferred_element_type=F32)


def dot_tn(left, right):
    return lax.dot_general(left, right, (((0,), (0,)), ((), ())), preferred_element_type=F32)


def column(ref):
    if len(ref.shape) == 3:
        return ref[0]
    senders, parts, _, own, channels = ref.shape
    return jnp.concatenate(
        [ref[:, n, 0].reshape(senders * own, channels) for n in range(parts)], axis=1
    )


def rows_kernel(x_ref, key_ref, first_ref, mixed_ref):
    scaled = (x_ref[0].astype(F32) * key_ref[...]).astype(BF)
    mixed_ref[0] = dot(first_ref[0], scaled).astype(BF)


def rows_back_kernel(bm_ref, x_ref, key_ref, first_ref, grad_ref, scaled_ref):
    back = bm_ref[0]
    scaled = (x_ref[0].astype(F32) * key_ref[...]).astype(BF)
    grad_ref[0] = dot_nt(back, scaled).astype(BF)
    scaled_ref[0] = dot_tn(first_ref[0], back).astype(BF)


def rows_grad_kernel(bm_ref, x_ref, key_ref, grad_ref):
    scaled = (x_ref[0].astype(F32) * key_ref[...]).astype(BF)
    grad_ref[0] = dot_nt(bm_ref[0], scaled).astype(BF)


def gate_part(mixed, second, x, gate):
    turned = dot(second, mixed).astype(BF).astype(F32)
    gate_pre = x * gate
    sig = logistic(gate_pre)
    hidden = (x + gate_pre * sig * turned).astype(BF)
    return turned, gate_pre, sig, hidden


def forward_kernel(second_ref, mixed_ref, x_ref, gate_ref, up1, up2, down1, down2, out_ref, sent):
    width = up2.shape[1]
    x = column(x_ref).astype(F32)
    _, _, _, hidden = gate_part(column(mixed_ref), second_ref[0], x, gate_ref[...])
    permuted = dot(hidden, up1[...]).astype(BF)
    folded = []
    for j in range(up2.shape[0]):
        pre = dot(permuted[:, j * width : (j + 1) * width], up2[j])
        active = (pre * logistic(pre)).astype(BF)
        folded.append(dot(active, down1[j]).astype(BF))
    folded = jnp.concatenate(folded, axis=1)
    result = (hidden.astype(F32) + dot(folded, down2[...])).astype(BF)
    out_ref[0] = result
    sent[0] = result


def backward_body(cot, mixed, second, x, gate, up1, up2, down1, down2):
    width = up2.shape[1]
    turned, gate_pre, sig, hidden = gate_part(mixed, second, x, gate)
    permuted = dot(hidden, up1[...]).astype(BF)
    back_fold = dot_nt(cot, down2[...]).astype(BF)
    back_perm = []
    for j in range(up2.shape[0]):
        cols = slice(j * width, (j + 1) * width)
        pre = dot(permuted[:, cols], up2[j])
        back_active = dot_nt(back_fold[:, cols], down1[j])
        act_sig = logistic(pre)
        back_pre = (back_active * (act_sig * (1.0 + pre * (1.0 - act_sig)))).astype(BF)
        back_perm.append(dot_nt(back_pre, up2[j]).astype(BF))
    back_perm = jnp.concatenate(back_perm, axis=1)
    back_hidden = cot.astype(F32) + dot_nt(back_perm, up1[...])
    back_turned = (back_hidden * (gate_pre * sig)).astype(BF)
    second_grad = dot_nt(back_turned, mixed).astype(BF)
    back_mixed = dot_tn(second, back_turned).astype(BF)
    direct = back_hidden + back_hidden * turned * (sig * (1.0 + gate_pre * (1.0 - sig))) * gate
    return second_grad, back_mixed, direct


def upper_kernel(
    second_ref, cot_ref, mixed_ref, x_ref, gate_ref, up1, up2, down1, down2,
    grad_ref, direct_ref, back_ref,
):
    x = x_ref[0].astype(F32)
    grad_ref[0], back_ref[0], direct_ref[0] = backward_body(
        column(cot_ref), mixed_ref[0], second_ref[0], x, gate_ref[...], up1, up2, down1, down2
    )


def lower_kernel(
    direct_ref, scaled_ref, key_ref, second_ref, mixed_ref, x_ref, gate_ref,
    up1, up2, down1, down2, grad_ref, back_ref,
):
    x = column(x_ref).astype(F32)
    cot = (direct_ref[0] + scaled_ref[0].astype(F32) * key_ref[...]).astype(BF)
    grad_ref[0], back_ref[0], _ = backward_body(
        cot, column(mixed_ref), second_ref[0], x, gate_ref[...], up1, up2, down1, down2
    )


def blocked(shape):
    return pl.BlockSpec((1,) + tuple(shape[1:]), lambda n: (n,) + (0,) * (len(shape) - 1))


def whole(shape):
    return pl.BlockSpec(tuple(shape), lambda n: (0,) * len(shape))


def spec(shape, how):
    if how is True and len(shape) == 5:
        return pl.BlockSpec((shape[0], shape[1], 1) + tuple(shape[3:]), lambda n: (0, 0, n, 0, 0))
    if how is True:
        return blocked(shape)
    if how is False:
        return whole(shape)
    layer = how[0]
    return pl.BlockSpec((None,) + tuple(shape[1:]), lambda n: (layer,) + (0,) * (len(shape) - 1))


def run(kernel, steps, operands, outs, flops):
    moved = sum(a.size * a.dtype.itemsize for a, _ in operands)
    moved += sum(int(jnp.dtype(d).itemsize) * functools.reduce(lambda p, q: p * q, s) for s, d in outs)
    result = pl.pallas_call(
        kernel,
        grid=(steps,),
        in_specs=[spec(a.shape, how) for a, how in operands],
        out_specs=[blocked(s) for s, _ in outs],
        out_shape=[jax.ShapeDtypeStruct(s, d) for s, d in outs],
        cost_estimate=pl.CostEstimate(flops=flops, bytes_accessed=moved, transcendentals=0),
        compiler_params=pltpu.CompilerParams(
            vmem_limit_bytes=VMEM_LIMIT, dimension_semantics=("arbitrary",)
        ),
    )(*[a for a, _ in operands])
    return result


class Outgoing:
    def __init__(self, ref, step):
        self.ref, self.step = ref, step

    def __setitem__(self, _, rows):
        count, _, own, channels = self.ref.shape
        self.ref[:, self.step] = rows.reshape(count, own, channels)


class Handed:
    def __init__(self, ref, step):
        self.ref, self.step = ref, step

    def __setitem__(self, _, grad):
        self.ref[self.step] = grad


def run_and_send(kernel, steps, operands, outs, flops, collective_id, channels=0, layer=None, group=1):
    parts, segments, seqs = lax.axis_size("mp"), lax.axis_size("segment"), lax.axis_size("seq")
    count = parts * segments * seqs
    near = parts * segments
    own = steps
    group = min(group, own)
    size = operands[0][0].shape[1]
    half = size // parts
    n_in, n_out = len(operands), len(outs)
    turns, hands = channels > 0, layer is not None

    def body(*refs):
        refs = list(refs)
        ins, refs = refs[:n_in], refs[n_in:]
        local, refs = refs[:n_out], refs[n_out:]
        got = refs.pop(0) if turns else None
        grads = refs.pop(0) if hands else None
        if turns:
            slots, send_sem, recv_sem, own_sem = refs[:4]
            refs = refs[4:]
        if hands:
            held, grad_send, grad_recv, grad_own = refs
        step = pl.program_id(0)
        segment, part = lax.axis_index("segment"), lax.axis_index("mp")
        me_near = segment * parts + part
        me = lax.axis_index("seq") * near + me_near
        met = count if turns else near

        def place(k):
            if not turns:
                device = lax.rem(me_near + k, near)
                return device, {"segment": device // parts, "mp": lax.rem(device, parts)}
            device = lax.rem(me + k, count)
            return device, {
                "segment": lax.rem(device // parts, segments),
                "seq": device // near,
                "mp": lax.rem(device, parts),
            }

        barrier = pltpu.get_barrier_semaphore()

        @pl.when(step == 0)
        def _():
            @pl.loop(1, met)
            def _(k):
                pl.semaphore_signal(
                    barrier, inc=1, device_id=place(k)[1], device_id_type=pl.DeviceIdType.MESH
                )

        kernel(
            *ins,
            *([Handed(held, step)] if hands else []),
            *local,
            *([Outgoing(slots, step)] if turns else []),
        )

        @pl.when(step == group - 1)
        def _():
            pl.semaphore_wait(barrier, met - 1)

        @pl.when(lax.rem(step, group) == group - 1)
        def _():
            base = step - (group - 1)
            if turns:
                target = got.at[pl.ds(me * own + base, group)]

                @pl.loop(1, count)
                def _(k):
                    device, where = place(k)
                    pltpu.make_async_remote_copy(
                        src_ref=slots.at[device, pl.ds(base, group)],
                        dst_ref=target,
                        send_sem=send_sem,
                        recv_sem=recv_sem,
                        device_id=where,
                        device_id_type=pl.DeviceIdType.MESH,
                    ).start()

            if hands:
                for h in range(parts):

                    @pl.when(me_near != layer * parts + h)
                    def _():
                        pltpu.make_async_remote_copy(
                            src_ref=held.at[pl.ds(base, group), pl.ds(h * half, half)],
                            dst_ref=grads.at[me_near, pl.ds(base, group)],
                            send_sem=grad_send,
                            recv_sem=grad_recv,
                            device_id={"segment": layer, "mp": h},
                            device_id_type=pl.DeviceIdType.MESH,
                        ).start()

        @pl.when(step == own - 1)
        def _():
            if hands:
                for h in range(parts):

                    @pl.when(me_near == layer * parts + h)
                    def _():
                        mine = pltpu.make_async_copy(
                            held.at[:, pl.ds(h * half, half)], grads.at[layer * parts + h], grad_own
                        )
                        mine.start()
                        mine.wait()

            if turns:
                mine = pltpu.make_async_copy(slots.at[me], got.at[pl.ds(me * own, own)], own_sem)
                mine.start()
                mine.wait()
                others = slots.at[pl.ds(0, count - 1)]
                pltpu.make_async_copy(others, others, send_sem).wait()
                arrived = got.at[pl.ds(0, (count - 1) * own)]
                pltpu.make_async_copy(arrived, arrived, recv_sem).wait()
            if hands:

                @pl.when(segment == layer)
                def _():
                    if parts > 1:
                        some = held.at[:, pl.ds(0, (parts - 1) * half)]
                        pltpu.make_async_copy(some, some, grad_send).wait()
                    arrived = grads.at[pl.ds(0, near - 1)]
                    pltpu.make_async_copy(arrived, arrived, grad_recv).wait()

                @pl.when(segment != layer)
                def _():
                    pltpu.make_async_copy(held, held, grad_send).wait()

    any_place = pl.BlockSpec(memory_space=pl.ANY)
    specs = [blocked(s) for s, _ in outs]
    shapes = [jax.ShapeDtypeStruct(s, d) for s, d in outs]
    scratch = []
    if turns:
        specs.append(any_place)
        shapes.append(jax.ShapeDtypeStruct((count * own, own, channels), BF))
        scratch += [pltpu.VMEM((count, own, own, channels), BF)] + [pltpu.SemaphoreType.DMA] * 3
    if hands:
        specs.append(any_place)
        shapes.append(jax.ShapeDtypeStruct((near, own, half, size), BF))
        scratch += [pltpu.VMEM((own, size, size), BF)] + [pltpu.SemaphoreType.DMA] * 3
    moved = sum(a.size * a.dtype.itemsize for a, _ in operands)
    result = list(
        pl.pallas_call(
            body,
            grid=(steps,),
            in_specs=[spec(a.shape, how) for a, how in operands],
            out_specs=specs,
            out_shape=shapes,
            scratch_shapes=scratch,
            cost_estimate=pl.CostEstimate(
                flops=flops, bytes_accessed=moved + 150_000_000, transcendentals=0
            ),
            compiler_params=pltpu.CompilerParams(
                vmem_limit_bytes=VMEM_LIMIT, dimension_semantics=("arbitrary",),
                collective_id=collective_id, has_side_effects=True,
            ),
        )(*[a for a, _ in operands])
    )
    if turns:
        result[n_out] = jnp.swapaxes(result[n_out], 0, 1)
    return result


def order_columns(rows):
    return jnp.swapaxes(rows, 0, 1)


def turn_split(sent):
    full, own, channels = sent.shape
    count = lax.axis_size(ALL)
    parts = lax.axis_size("mp")
    got = lax.all_to_all(sent, ALL, split_axis=0, concat_axis=0, tiled=True)
    got = got.reshape(count // parts, parts, full // count, own, channels)
    if own % 16 == 0:
        return got
    return jnp.transpose(got, (2, 0, 3, 1, 4)).reshape(
        full // count, count // parts * own, parts * channels
    )


def swap(pieces, axis):
    count = lax.axis_size(axis)
    me = lax.axis_index(axis)

    def chosen(index):
        piece = pieces[0]
        for n in range(1, count):
            piece = jnp.where(index == n, pieces[n], piece)
        return piece

    held = [chosen(me)]
    for shift in range(1, count):
        route = [(n, (n + shift) % count) for n in range(count)]
        held.append(lax.ppermute(chosen((me + shift) % count), axis, route))
    result = []
    for source in range(count):
        piece = held[0]
        for shift in range(1, count):
            piece = jnp.where((me - source) % count == shift, held[shift], piece)
        result.append(piece)
    return result


def spread_pair(first, last):
    layers, blocks, width, _ = first.shape
    sub = width // blocks
    row = lax.broadcasted_iota(jnp.int32, (blocks, width, blocks * width), 1)
    col = lax.broadcasted_iota(jnp.int32, (blocks, width, blocks * width), 2)
    block = lax.broadcasted_iota(jnp.int32, (blocks, width, blocks * width), 0)
    place = (row // sub) * width + block * sub + row % sub
    spread = (col == place).astype(BF)
    up = jnp.einsum("lkir,krn->lkin", first, spread, preferred_element_type=F32)
    down = jnp.einsum("krn,lkrf->lnkf", spread, last, preferred_element_type=F32)
    full = blocks * width
    return up.astype(BF).reshape(layers, full, full), down.astype(BF).reshape(layers, full, full)


def on_device(
    inputs, cotangent, gate_gain, key_gain, first_factor, second_factor,
    up_first, up_second, down_first, down_second_weight,
):
    segments = lax.axis_size("segment")
    parts = lax.axis_size("mp")
    segment = lax.axis_index("segment")
    part = lax.axis_index("mp")
    size = first_factor.shape[2]
    held = first_factor.shape[1]
    channels = inputs.shape[1]
    model = channels * parts
    core_rows = held // segments
    own = core_rows // parts

    gains = jnp.concatenate([key_gain, gate_gain], axis=0)
    gains = lax.all_gather(gains, ("segment", "mp"), axis=0, tiled=False)
    gains = jnp.transpose(gains.reshape(segments, parts, 2, channels), (2, 0, 1, 3))
    gains = gains.reshape(2, segments, 1, model)
    keys, gates = gains[0], gains[1]

    first_cut = first_factor.reshape(segments, core_rows, size, size)
    first_low, first_high = swap([first_cut[n] for n in range(segments)], "segment")
    first_high = lax.dynamic_slice_in_dim(first_high, part * own, own, 0)
    second_mine = lax.dynamic_index_in_dim(
        second_factor.reshape(segments, parts, own, size, size), part, 1, keepdims=False
    )
    second_low_block, second_high_block = swap(
        [second_mine[n] for n in range(segments)], "segment"
    )

    core_in = lax.dynamic_slice_in_dim(
        inputs.reshape(held, size, channels), segment * core_rows, core_rows, 0
    )
    core_cot = lax.dynamic_slice_in_dim(
        cotangent.reshape(held, size, channels), segment * core_rows, core_rows, 0
    )

    blocks = up_first.shape[1]
    width = up_first.shape[2]
    packed = jnp.concatenate(
        [
            a.reshape(blocks, -1, width)
            for a in (up_first[0], up_second[0], down_first[0], down_second_weight[0])
        ],
        axis=1,
    )
    packed = lax.all_gather(packed, ("segment", "mp"), axis=0, tiled=False)
    packed = packed.reshape(segments, parts * blocks, -1, width)
    hidden = up_second.shape[3]
    cuts = (0, width, width + hidden, width + 2 * hidden, 2 * width + 2 * hidden)
    piece = [packed[:, :, cuts[n] : cuts[n + 1]] for n in range(4)]
    ups = piece[1].reshape(segments, parts * blocks, width, hidden)
    downs = piece[2]
    wide_up, wide_down = spread_pair(piece[0], piece[3])

    def ffn(layer):
        return [
            (wide_up, (layer,)), (ups, (layer,)), (downs, (layer,)), (wide_down, (layer,)),
        ]

    grid_rows = (own, size, model)
    grad_shape = (own, size, size)
    cube = 2 * own * size * size * model
    feed = 2 * own * size * model * (2 * model + 2 * hidden)

    key_low = lax.dynamic_slice_in_dim(keys[0], part * channels, channels, 1)
    (mixed_low,) = run(
        rows_kernel, core_rows,
        [(core_in, True), (key_low, False), (first_low, True)],
        [((core_rows, size, channels), BF)], cube,
    )
    in_cols = turn_split(order_columns(core_in))
    mixed_low, in_cols = lax.optimization_barrier((order_columns(mixed_low), in_cols))
    mixed_low = turn_split(mixed_low)
    cot_cols = turn_split(order_columns(core_cot))
    middle, middle_rows = run_and_send(
        forward_kernel, own,
        [(second_low_block, True), (mixed_low, True), (in_cols, True), (gates[0], False)] + ffn(0),
        [(grid_rows, BF)], cube + feed, 0, channels=model,
    )
    middle_rows, cot_cols = lax.optimization_barrier((middle_rows, cot_cols))
    (mixed_high,) = run_and_send(
        rows_kernel, own,
        [(middle_rows, True), (keys[1], False), (first_high, True)],
        [], cube, 1, channels=model, group=2,
    )
    direct, back_rows, second_high = run_and_send(
        upper_kernel, own,
        [
            (second_high_block, True), (cot_cols, True), (mixed_high, True),
            (middle, True), (gates[1], False),
        ] + ffn(1),
        [(grid_rows, F32)], 3 * cube + 2 * feed, 2, channels=model, layer=1,
    )
    scaled_cols, grad_high = run_and_send(
        rows_back_kernel, own,
        [(back_rows, True), (middle_rows, True), (keys[1], False), (first_high, True)],
        [], 2 * cube, 3, channels=model, layer=1, group=2,
    )
    in_cut = core_in.reshape(parts, own, size, channels)
    in_rows = jnp.concatenate(swap([in_cut[n] for n in range(parts)], "mp"), axis=2)
    scaled_cols, in_rows = lax.optimization_barrier((scaled_cols, in_rows))
    low_rows, second_low = run_and_send(
        lower_kernel, own,
        [
            (direct, True), (scaled_cols, True), (keys[1], False), (second_low_block, True),
            (mixed_low, True), (in_cols, True), (gates[0], False),
        ] + ffn(0),
        [], 3 * cube + 2 * feed, 4, channels=model, layer=0,
    )

    def result(low, high):
        chosen = jnp.where(segment == 0, low, high)
        return chosen.reshape(1, held, size // parts, size).astype(F32)

    second_out = result(second_low, second_high)
    low_rows, second_out = lax.optimization_barrier((low_rows, second_out))
    (grad_low,) = run_and_send(
        rows_grad_kernel, own,
        [(low_rows, True), (in_rows, True), (keys[0], False)],
        [], cube, 5, layer=0, group=2,
    )
    return result(grad_low, grad_high), second_out


def solution(mesh):
    placed = (
        P("seq", "mp"),
        P("seq", "mp"),
        P("segment", "mp"),
        P("segment", "mp"),
        P("segment", "seq", None, None),
        P("segment", "seq", None, None),
        P("segment", "mp", None, None),
        P("segment", "mp", None, None),
        P("segment", "mp", None, None),
        P("segment", "mp", None, None),
    )
    return jax.shard_map(
        on_device,
        mesh=mesh,
        in_specs=placed,
        out_specs=(P("segment", "seq", "mp", None), P("segment", "seq", "mp", None)),
        check_vma=False,
    )
```

```python
import functools

import jax
import jax.numpy as jnp
from jax import lax
from jax.experimental import pallas as pl
from jax.experimental.pallas import tpu as pltpu
from jax.sharding import PartitionSpec as P

ALL = ("seq", "segment", "mp")
VMEM_LIMIT = 48 * 1024 * 1024
BF = jnp.bfloat16
F32 = jnp.float32


def logistic(values):
    return 0.5 + 0.5 * jnp.tanh(0.5 * values)


def dot(left, right):
    return lax.dot_general(left, right, (((1,), (0,)), ((), ())), preferred_element_type=F32)


def dot_nt(left, right):
    return lax.dot_general(left, right, (((1,), (1,)), ((), ())), preferred_element_type=F32)


def dot_tn(left, right):
    return lax.dot_general(left, right, (((0,), (0,)), ((), ())), preferred_element_type=F32)


def column(ref):
    if len(ref.shape) == 3:
        return ref[0]
    senders, parts, _, own, channels = ref.shape
    return jnp.concatenate(
        [ref[:, n, 0].reshape(senders * own, channels) for n in range(parts)], axis=1
    )


def rows_kernel(x_ref, key_ref, first_ref, mixed_ref):
    scaled = (x_ref[0].astype(F32) * key_ref[...]).astype(BF)
    mixed_ref[0] = dot(first_ref[0], scaled).astype(BF)


def rows_back_kernel(bm_ref, x_ref, key_ref, first_ref, grad_ref, scaled_ref):
    back = bm_ref[0]
    scaled = (x_ref[0].astype(F32) * key_ref[...]).astype(BF)
    grad_ref[0] = dot_nt(back, scaled).astype(BF)
    scaled_ref[0] = dot_tn(first_ref[0], back).astype(BF)


def rows_grad_kernel(bm_ref, x_ref, key_ref, grad_ref):
    scaled = (x_ref[0].astype(F32) * key_ref[...]).astype(BF)
    grad_ref[0] = dot_nt(bm_ref[0], scaled).astype(BF)


def gate_part(mixed, second, x, gate):
    turned = dot(second, mixed).astype(BF).astype(F32)
    gate_pre = x * gate
    sig = logistic(gate_pre)
    hidden = (x + gate_pre * sig * turned).astype(BF)
    return turned, gate_pre, sig, hidden


def forward_kernel(second_ref, mixed_ref, x_ref, gate_ref, up1, up2, down1, down2, out_ref, sent):
    width = up2.shape[1]
    x = column(x_ref).astype(F32)
    _, _, _, hidden = gate_part(column(mixed_ref), second_ref[0], x, gate_ref[...])
    permuted = dot(hidden, up1[...]).astype(BF)
    folded = []
    for j in range(up2.shape[0]):
        pre = dot(permuted[:, j * width : (j + 1) * width], up2[j])
        active = (pre * logistic(pre)).astype(BF)
        folded.append(dot(active, down1[j]).astype(BF))
    folded = jnp.concatenate(folded, axis=1)
    result = (hidden.astype(F32) + dot(folded, down2[...])).astype(BF)
    out_ref[0] = result
    sent[0] = result


def backward_body(cot, mixed, second, x, gate, up1, up2, down1, down2):
    width = up2.shape[1]
    turned, gate_pre, sig, hidden = gate_part(mixed, second, x, gate)
    permuted = dot(hidden, up1[...]).astype(BF)
    back_fold = dot_nt(cot, down2[...]).astype(BF)
    back_perm = []
    for j in range(up2.shape[0]):
        cols = slice(j * width, (j + 1) * width)
        pre = dot(permuted[:, cols], up2[j])
        back_active = dot_nt(back_fold[:, cols], down1[j])
        act_sig = logistic(pre)
        back_pre = (back_active * (act_sig * (1.0 + pre * (1.0 - act_sig)))).astype(BF)
        back_perm.append(dot_nt(back_pre, up2[j]).astype(BF))
    back_perm = jnp.concatenate(back_perm, axis=1)
    back_hidden = cot.astype(F32) + dot_nt(back_perm, up1[...])
    back_turned = (back_hidden * (gate_pre * sig)).astype(BF)
    second_grad = dot_nt(back_turned, mixed).astype(BF)
    back_mixed = dot_tn(second, back_turned).astype(BF)
    direct = back_hidden + back_hidden * turned * (sig * (1.0 + gate_pre * (1.0 - sig))) * gate
    return second_grad, back_mixed, direct


def upper_kernel(
    second_ref, cot_ref, mixed_ref, x_ref, gate_ref, up1, up2, down1, down2,
    grad_ref, direct_ref, back_ref,
):
    x = x_ref[0].astype(F32)
    grad_ref[0], back_ref[0], direct_ref[0] = backward_body(
        column(cot_ref), mixed_ref[0], second_ref[0], x, gate_ref[...], up1, up2, down1, down2
    )


def lower_kernel(
    direct_ref, scaled_ref, key_ref, second_ref, mixed_ref, x_ref, gate_ref,
    up1, up2, down1, down2, grad_ref, back_ref,
):
    x = column(x_ref).astype(F32)
    cot = (direct_ref[0] + scaled_ref[0].astype(F32) * key_ref[...]).astype(BF)
    grad_ref[0], back_ref[0], _ = backward_body(
        cot, column(mixed_ref), second_ref[0], x, gate_ref[...], up1, up2, down1, down2
    )


def blocked(shape):
    return pl.BlockSpec((1,) + tuple(shape[1:]), lambda n: (n,) + (0,) * (len(shape) - 1))


def whole(shape):
    return pl.BlockSpec(tuple(shape), lambda n: (0,) * len(shape))


def spec(shape, how):
    if how is True and len(shape) == 5:
        return pl.BlockSpec((shape[0], shape[1], 1) + tuple(shape[3:]), lambda n: (0, 0, n, 0, 0))
    if how is True:
        return blocked(shape)
    if how is False:
        return whole(shape)
    layer = how[0]
    return pl.BlockSpec((None,) + tuple(shape[1:]), lambda n: (layer,) + (0,) * (len(shape) - 1))


def run(kernel, steps, operands, outs, flops):
    moved = sum(a.size * a.dtype.itemsize for a, _ in operands)
    moved += sum(int(jnp.dtype(d).itemsize) * functools.reduce(lambda p, q: p * q, s) for s, d in outs)
    result = pl.pallas_call(
        kernel,
        grid=(steps,),
        in_specs=[spec(a.shape, how) for a, how in operands],
        out_specs=[blocked(s) for s, _ in outs],
        out_shape=[jax.ShapeDtypeStruct(s, d) for s, d in outs],
        cost_estimate=pl.CostEstimate(flops=flops, bytes_accessed=moved, transcendentals=0),
        compiler_params=pltpu.CompilerParams(
            vmem_limit_bytes=VMEM_LIMIT, dimension_semantics=("arbitrary",)
        ),
    )(*[a for a, _ in operands])
    return result


class Outgoing:
    def __init__(self, ref, step):
        self.ref, self.step = ref, step

    def __setitem__(self, _, rows):
        count, _, own, channels = self.ref.shape
        self.ref[:, self.step] = rows.reshape(count, own, channels)


class Handed:
    def __init__(self, ref, step):
        self.ref, self.step = ref, step

    def __setitem__(self, _, grad):
        self.ref[self.step] = grad


def run_and_send(kernel, steps, operands, outs, flops, collective_id, channels=0, layer=None, group=2):
    parts, segments, seqs = lax.axis_size("mp"), lax.axis_size("segment"), lax.axis_size("seq")
    count = parts * segments * seqs
    near = parts * segments
    own = steps
    group = min(group, own)
    size = operands[0][0].shape[1]
    half = size // parts
    n_in, n_out = len(operands), len(outs)
    turns, hands = channels > 0, layer is not None

    def body(*refs):
        refs = list(refs)
        ins, refs = refs[:n_in], refs[n_in:]
        local, refs = refs[:n_out], refs[n_out:]
        got = refs.pop(0) if turns else None
        grads = refs.pop(0) if hands else None
        if turns:
            slots, send_sem, recv_sem, own_sem = refs[:4]
            refs = refs[4:]
        if hands:
            held, grad_send, grad_recv, grad_own = refs
        step = pl.program_id(0)
        segment, part = lax.axis_index("segment"), lax.axis_index("mp")
        me_near = segment * parts + part
        me = lax.axis_index("seq") * near + me_near
        met = count if turns else near

        def place(k):
            if not turns:
                device = lax.rem(me_near + k, near)
                return device, {"segment": device // parts, "mp": lax.rem(device, parts)}
            device = lax.rem(me + k, count)
            return device, {
                "segment": lax.rem(device // parts, segments),
                "seq": device // near,
                "mp": lax.rem(device, parts),
            }

        barrier = pltpu.get_barrier_semaphore()

        @pl.when(step == 0)
        def _():
            @pl.loop(1, met)
            def _(k):
                pl.semaphore_signal(
                    barrier, inc=1, device_id=place(k)[1], device_id_type=pl.DeviceIdType.MESH
                )

        kernel(
            *ins,
            *([Handed(held, step)] if hands else []),
            *local,
            *([Outgoing(slots, step)] if turns else []),
        )

        @pl.when(step == group - 1)
        def _():
            pl.semaphore_wait(barrier, met - 1)

        @pl.when(lax.rem(step, group) == group - 1)
        def _():
            base = step - (group - 1)
            if turns:
                target = got.at[pl.ds(me * own + base, group)]

                @pl.loop(1, count)
                def _(k):
                    device, where = place(k)
                    pltpu.make_async_remote_copy(
                        src_ref=slots.at[device, pl.ds(base, group)],
                        dst_ref=target,
                        send_sem=send_sem,
                        recv_sem=recv_sem,
                        device_id=where,
                        device_id_type=pl.DeviceIdType.MESH,
                    ).start()

            if hands:
                for h in range(parts):

                    @pl.when(me_near != layer * parts + h)
                    def _():
                        pltpu.make_async_remote_copy(
                            src_ref=held.at[pl.ds(base, group), pl.ds(h * half, half)],
                            dst_ref=grads.at[me_near, pl.ds(base, group)],
                            send_sem=grad_send,
                            recv_sem=grad_recv,
                            device_id={"segment": layer, "mp": h},
                            device_id_type=pl.DeviceIdType.MESH,
                        ).start()

        @pl.when(step == own - 1)
        def _():
            if hands:
                for h in range(parts):

                    @pl.when(me_near == layer * parts + h)
                    def _():
                        mine = pltpu.make_async_copy(
                            held.at[:, pl.ds(h * half, half)], grads.at[layer * parts + h], grad_own
                        )
                        mine.start()
                        mine.wait()

            if turns:
                mine = pltpu.make_async_copy(slots.at[me], got.at[pl.ds(me * own, own)], own_sem)
                mine.start()
                mine.wait()
                others = slots.at[pl.ds(0, count - 1)]
                pltpu.make_async_copy(others, others, send_sem).wait()
                arrived = got.at[pl.ds(0, (count - 1) * own)]
                pltpu.make_async_copy(arrived, arrived, recv_sem).wait()
            if hands:

                @pl.when(segment == layer)
                def _():
                    if parts > 1:
                        some = held.at[:, pl.ds(0, (parts - 1) * half)]
                        pltpu.make_async_copy(some, some, grad_send).wait()
                    arrived = grads.at[pl.ds(0, near - 1)]
                    pltpu.make_async_copy(arrived, arrived, grad_recv).wait()

                @pl.when(segment != layer)
                def _():
                    pltpu.make_async_copy(held, held, grad_send).wait()

    any_place = pl.BlockSpec(memory_space=pl.ANY)
    specs = [blocked(s) for s, _ in outs]
    shapes = [jax.ShapeDtypeStruct(s, d) for s, d in outs]
    scratch = []
    if turns:
        specs.append(any_place)
        shapes.append(jax.ShapeDtypeStruct((count * own, own, channels), BF))
        scratch += [pltpu.VMEM((count, own, own, channels), BF)] + [pltpu.SemaphoreType.DMA] * 3
    if hands:
        specs.append(any_place)
        shapes.append(jax.ShapeDtypeStruct((near, own, half, size), BF))
        scratch += [pltpu.VMEM((own, size, size), BF)] + [pltpu.SemaphoreType.DMA] * 3
    moved = sum(a.size * a.dtype.itemsize for a, _ in operands)
    result = list(
        pl.pallas_call(
            body,
            grid=(steps,),
            in_specs=[spec(a.shape, how) for a, how in operands],
            out_specs=specs,
            out_shape=shapes,
            scratch_shapes=scratch,
            cost_estimate=pl.CostEstimate(
                flops=flops, bytes_accessed=moved + 150_000_000, transcendentals=0
            ),
            compiler_params=pltpu.CompilerParams(
                vmem_limit_bytes=VMEM_LIMIT, dimension_semantics=("arbitrary",),
                collective_id=collective_id, has_side_effects=True,
            ),
        )(*[a for a, _ in operands])
    )
    if turns:
        result[n_out] = jnp.swapaxes(result[n_out], 0, 1)
    return result


def order_columns(rows):
    return jnp.swapaxes(rows, 0, 1)


def turn_split(sent):
    full, own, channels = sent.shape
    count = lax.axis_size(ALL)
    parts = lax.axis_size("mp")
    got = lax.all_to_all(sent, ALL, split_axis=0, concat_axis=0, tiled=True)
    got = got.reshape(count // parts, parts, full // count, own, channels)
    if own % 16 == 0:
        return got
    return jnp.transpose(got, (2, 0, 3, 1, 4)).reshape(
        full // count, count // parts * own, parts * channels
    )


def swap(pieces, axis):
    count = lax.axis_size(axis)
    me = lax.axis_index(axis)

    def chosen(index):
        piece = pieces[0]
        for n in range(1, count):
            piece = jnp.where(index == n, pieces[n], piece)
        return piece

    held = [chosen(me)]
    for shift in range(1, count):
        route = [(n, (n + shift) % count) for n in range(count)]
        held.append(lax.ppermute(chosen((me + shift) % count), axis, route))
    result = []
    for source in range(count):
        piece = held[0]
        for shift in range(1, count):
            piece = jnp.where((me - source) % count == shift, held[shift], piece)
        result.append(piece)
    return result


def spread_pair(first, last):
    layers, blocks, width, _ = first.shape
    sub = width // blocks
    row = lax.broadcasted_iota(jnp.int32, (blocks, width, blocks * width), 1)
    col = lax.broadcasted_iota(jnp.int32, (blocks, width, blocks * width), 2)
    block = lax.broadcasted_iota(jnp.int32, (blocks, width, blocks * width), 0)
    place = (row // sub) * width + block * sub + row % sub
    spread = (col == place).astype(BF)
    up = jnp.einsum("lkir,krn->lkin", first, spread, preferred_element_type=F32)
    down = jnp.einsum("krn,lkrf->lnkf", spread, last, preferred_element_type=F32)
    full = blocks * width
    return up.astype(BF).reshape(layers, full, full), down.astype(BF).reshape(layers, full, full)


def on_device(
    inputs, cotangent, gate_gain, key_gain, first_factor, second_factor,
    up_first, up_second, down_first, down_second_weight,
):
    segments = lax.axis_size("segment")
    parts = lax.axis_size("mp")
    segment = lax.axis_index("segment")
    part = lax.axis_index("mp")
    size = first_factor.shape[2]
    held = first_factor.shape[1]
    channels = inputs.shape[1]
    model = channels * parts
    core_rows = held // segments
    own = core_rows // parts

    gains = jnp.concatenate([key_gain, gate_gain], axis=0)
    gains = lax.all_gather(gains, ("segment", "mp"), axis=0, tiled=False)
    gains = jnp.transpose(gains.reshape(segments, parts, 2, channels), (2, 0, 1, 3))
    gains = gains.reshape(2, segments, 1, model)
    keys, gates = gains[0], gains[1]

    first_cut = first_factor.reshape(segments, core_rows, size, size)
    first_low, first_high = swap([first_cut[n] for n in range(segments)], "segment")
    first_high = lax.dynamic_slice_in_dim(first_high, part * own, own, 0)
    second_mine = lax.dynamic_index_in_dim(
        second_factor.reshape(segments, parts, own, size, size), part, 1, keepdims=False
    )
    second_low_block, second_high_block = swap(
        [second_mine[n] for n in range(segments)], "segment"
    )

    core_in = lax.dynamic_slice_in_dim(
        inputs.reshape(held, size, channels), segment * core_rows, core_rows, 0
    )
    core_cot = lax.dynamic_slice_in_dim(
        cotangent.reshape(held, size, channels), segment * core_rows, core_rows, 0
    )

    blocks = up_first.shape[1]
    width = up_first.shape[2]
    packed = jnp.concatenate(
        [
            a.reshape(blocks, -1, width)
            for a in (up_first[0], up_second[0], down_first[0], down_second_weight[0])
        ],
        axis=1,
    )
    packed = lax.all_gather(packed, ("segment", "mp"), axis=0, tiled=False)
    packed = packed.reshape(segments, parts * blocks, -1, width)
    hidden = up_second.shape[3]
    cuts = (0, width, width + hidden, width + 2 * hidden, 2 * width + 2 * hidden)
    piece = [packed[:, :, cuts[n] : cuts[n + 1]] for n in range(4)]
    ups = piece[1].reshape(segments, parts * blocks, width, hidden)
    downs = piece[2]
    wide_up, wide_down = spread_pair(piece[0], piece[3])

    def ffn(layer):
        return [
            (wide_up, (layer,)), (ups, (layer,)), (downs, (layer,)), (wide_down, (layer,)),
        ]

    grid_rows = (own, size, model)
    grad_shape = (own, size, size)
    cube = 2 * own * size * size * model
    feed = 2 * own * size * model * (2 * model + 2 * hidden)

    key_low = lax.dynamic_slice_in_dim(keys[0], part * channels, channels, 1)
    (mixed_low,) = run(
        rows_kernel, core_rows,
        [(core_in, True), (key_low, False), (first_low, True)],
        [((core_rows, size, channels), BF)], cube,
    )
    in_cols = turn_split(order_columns(core_in))
    mixed_low, in_cols = lax.optimization_barrier((order_columns(mixed_low), in_cols))
    mixed_low = turn_split(mixed_low)
    cot_cols = turn_split(order_columns(core_cot))
    middle, middle_rows = run_and_send(
        forward_kernel, own,
        [(second_low_block, True), (mixed_low, True), (in_cols, True), (gates[0], False)] + ffn(0),
        [(grid_rows, BF)], cube + feed, 0, channels=model,
    )
    middle_rows, cot_cols = lax.optimization_barrier((middle_rows, cot_cols))
    (mixed_high,) = run_and_send(
        rows_kernel, own,
        [(middle_rows, True), (keys[1], False), (first_high, True)],
        [], cube, 1, channels=model,
    )
    mixed_high, core_late = lax.optimization_barrier((mixed_high, core_in))
    direct, back_rows, second_high = run_and_send(
        upper_kernel, own,
        [
            (second_high_block, True), (cot_cols, True), (mixed_high, True),
            (middle, True), (gates[1], False),
        ] + ffn(1),
        [(grid_rows, F32)], 3 * cube + 2 * feed, 2, channels=model, layer=1,
    )
    scaled_cols, grad_high = run_and_send(
        rows_back_kernel, own,
        [(back_rows, True), (middle_rows, True), (keys[1], False), (first_high, True)],
        [], 2 * cube, 3, channels=model, layer=1,
    )
    in_cut = core_late.reshape(parts, own, size, channels)
    in_rows = jnp.concatenate(swap([in_cut[n] for n in range(parts)], "mp"), axis=2)
    scaled_cols, in_rows = lax.optimization_barrier((scaled_cols, in_rows))
    low_rows, second_low = run_and_send(
        lower_kernel, own,
        [
            (direct, True), (scaled_cols, True), (keys[1], False), (second_low_block, True),
            (mixed_low, True), (in_cols, True), (gates[0], False),
        ] + ffn(0),
        [], 3 * cube + 2 * feed, 4, channels=model, layer=0,
    )

    def result(low, high):
        chosen = jnp.where(segment == 0, low, high)
        return chosen.reshape(1, held, size // parts, size).astype(F32)

    second_out = result(second_low, second_high)
    low_rows, second_out = lax.optimization_barrier((low_rows, second_out))
    (grad_low,) = run_and_send(
        rows_grad_kernel, own,
        [(low_rows, True), (in_rows, True), (keys[0], False)],
        [], cube, 5, layer=0,
    )
    return result(grad_low, grad_high), second_out


def solution(mesh):
    placed = (
        P("seq", "mp"),
        P("seq", "mp"),
        P("segment", "mp"),
        P("segment", "mp"),
        P("segment", "seq", None, None),
        P("segment", "seq", None, None),
        P("segment", "mp", None, None),
        P("segment", "mp", None, None),
        P("segment", "mp", None, None),
        P("segment", "mp", None, None),
    )
    return jax.shard_map(
        on_device,
        mesh=mesh,
        in_specs=placed,
        out_specs=(P("segment", "seq", "mp", None), P("segment", "seq", "mp", None)),
        check_vma=False,
    )
```
